768 devices in a mesh: dp: 96 (over y_hi, z, core), fsdp: 8 (over y_lo, x).
Axes of the slice: x: 4, y: 8 (y_hi: 4, y_lo: 2; y = y_hi * 2 + y_lo), z: 12, core: 2. Of those that a mesh axis runs over, the one named last changes fastest.
Arguments:
- features: bfloat16 [135168, 832], P(('dp', 'fsdp')), may hold values from -6 to 6
- head_weight: bfloat16 [832, 1024], P('fsdp'), may hold values from -0.21875 to 0.21875
- text_embed: bfloat16 [135168, 1024], P(('dp', 'fsdp')), may hold values from -1.5 to 1.5
Outputs:
- loss: float32 [], replicated
- feat_grad: bfloat16 [135168, 832], P(('dp', 'fsdp'))
- text_grad: bfloat16 [135168, 1024], P(('dp', 'fsdp'))
- head_grad: float32 [832, 1024], P('fsdp')
The draws below stay inside these ranges and needn't reach their ends.
All inputs are finite; a program needn't handle non-finite values.
Results may differ from the reference program's by a relative error of at most 0.011.
Values may be sent and summed in bfloat16 or wider, within the bound.
No kernel may reach another device: no remote copies, remote signals or barrier semaphores. Data moves between devices by JAX's collectives and lax.ppermute only.
A program may use at most 32 MiB of HBM per device.

```python
import jax
import jax.numpy as jnp
from jax import lax

DI = 832
E = 1024
GROUP = 1408
BATCH = 135168
N_DP = 96


def draw_text_embed(key, part):
    key = jax.random.fold_in(key, 11)
    first_key, second_key = jax.random.split(key, 2)
    position = jnp.arange(BATCH, dtype=jnp.float32) / float(max(BATCH - 1, 1))
    common = jax.random.normal(first_key, (N_DP, 1, E), jnp.float32)
    share = 0.85 * position
    own = jax.random.normal(second_key, (N_DP, GROUP, E), jnp.float32)
    share = share.reshape(N_DP, GROUP, 1)
    mixed = jnp.sqrt(share) * common + jnp.sqrt(1.0 - share) * own
    mixed = jnp.clip(0.25 * mixed, -1.5, 1.5)
    return mixed.reshape(BATCH, E).astype(jnp.bfloat16)


def shard_levels(rng, extent, pieces, least, top_value):
    def one(dim, blocks):
        heights = jax.random.uniform(jax.random.fold_in(jax.random.fold_in(rng, 6), dim), (blocks,), jnp.float32, least / len(pieces), top_value / len(pieces))
        return jnp.repeat(jnp.exp(heights), extent[dim] // blocks).reshape((-1,) + (1,) * (len(extent) - dim - 1))

    level = one(*pieces[0])
    for cut in pieces[1:]:
        level = level * one(*cut)
    return level


def gaussian(stream_key, shape, spread, reach, shards=(), kind=jnp.bfloat16):
    gain = shard_levels(stream_key, shape, shards, -0.22, 0.18) if shards else 1.0
    entries = jax.random.normal(stream_key, shape, jnp.float32) * spread * gain
    return jnp.minimum(jnp.maximum(entries, -reach), reach).astype(kind)


def setup_inputs(seed: int = 0) -> dict:
    arg_keys = jax.random.split(jax.random.key(seed), 4)
    return {
        "features": gaussian(arg_keys[0], (BATCH, DI), 1.0, 6.0, ((0, 768),)),
        "head_weight": gaussian(arg_keys[1], (DI, E), DI ** -0.5, 0.21875, ((0, 8),)),
        "text_embed": draw_text_embed(jax.random.fold_in(arg_keys[3], 71), 0),
    }


def unit_rows(vectors):
    inverse = lax.rsqrt(lax.optimization_barrier(jnp.sum(vectors * vectors, axis=-1, keepdims=True)) + 1e-06)
    return (vectors * inverse, inverse)

def reference(features, head_weight, text_embed):
    feat_groups = features.reshape(N_DP, GROUP, DI)
    text_groups = text_embed.reshape(N_DP, GROUP, E)
    identity = jnp.eye(GROUP, dtype=jnp.float32)

    def one_group(pair):
        feat_block, text_block = pair
        z_full = jnp.dot(feat_block, head_weight, preferred_element_type=jnp.float32)
        u_full, inv_u = unit_rows(z_full)
        image_unit = u_full.astype(jnp.bfloat16)
        v_full, inv_v = unit_rows(text_block.astype(jnp.float32))
        text_unit = v_full.astype(jnp.bfloat16)
        scores = 100.0 * jnp.dot(image_unit, text_unit.T, preferred_element_type=jnp.float32)
        lse_row = jax.scipy.special.logsumexp(scores, axis=1)
        lse_col = jax.scipy.special.logsumexp(scores, axis=0)
        diagonal = jnp.diagonal(scores)
        term = jnp.sum(lse_row - diagonal) + jnp.sum(lse_col - diagonal)
        coupling = (jnp.exp(scores - lse_row[:, None]) + jnp.exp(scores - lse_col[None, :]) - 2.0 * identity).astype(jnp.bfloat16)
        du_full = 100.0 * jnp.dot(coupling, text_unit, preferred_element_type=jnp.float32)
        dv_full = 100.0 * jnp.dot(coupling.T, image_unit, preferred_element_type=jnp.float32)
        dz_rows = ((du_full - u_full * lax.optimization_barrier(jnp.sum(u_full * du_full, axis=-1, keepdims=True))) * inv_u).astype(jnp.bfloat16)
        text_rows = ((dv_full - v_full * lax.optimization_barrier(jnp.sum(v_full * dv_full, axis=-1, keepdims=True))) * inv_v).astype(jnp.bfloat16)
        feat_rows = jnp.dot(dz_rows, head_weight.T, preferred_element_type=jnp.float32).astype(jnp.bfloat16)
        return (term, feat_rows, text_rows, dz_rows)
    terms, feat_rows, text_rows, dz_rows = lax.map(one_group, (feat_groups, text_groups))
    loss = jnp.sum(terms) / (2.0 * BATCH)
    head_grad = jnp.dot(features.T, dz_rows.reshape(BATCH, E), preferred_element_type=jnp.float32)
    return (loss, feat_rows.reshape(BATCH, DI), text_rows.reshape(BATCH, E), head_grad)
```

```python
import jax
import jax.numpy as jnp
from jax import lax
from jax.sharding import Mesh, PartitionSpec as P

BF = jnp.bfloat16
F32 = jnp.float32


def left_product(left, right):
    return lax.dot_general(
        left, right, (((0,), (0,)), ((), ())), preferred_element_type=F32
    )


def right_product(left, right):
    return lax.dot_general(
        left, right, (((1,), (1,)), ((), ())), preferred_element_type=F32
    )


def unit_rows(vectors):
    inverse = lax.rsqrt(jnp.sum(vectors * vectors, axis=-1, keepdims=True) + 1e-06)
    return (vectors * inverse, inverse)


def ring(size, step):
    return [(i, (i + step) % size) for i in range(size)]


def gather_group(block, n_y, n_x):
    flip, up, down = ring(n_y, 1), ring(n_x, 1), ring(n_x, -1)
    rows = block.shape[0]
    half = rows // 2 // 16 * 16
    got = {(0, 0): block}
    got[1, 0] = lax.ppermute(block, "yl", flip)
    got[0, 3] = lax.ppermute(block, "x", up)
    got[0, 1] = lax.ppermute(block, "x", down)
    got[1, 3] = lax.ppermute(got[0, 3], "yl", flip)
    got[1, 1] = lax.ppermute(got[1, 0], "x", down)
    got[0, 2] = lax.ppermute(got[0, 3], "x", up)
    low = lax.ppermute(got[1, 3][:half], "x", up)
    high = lax.ppermute(got[1, 1][half:], "x", down)
    got[1, 2] = jnp.concatenate([low, high], axis=0)
    return got


def compute(weight, features, texts, own, columns):
    group = features.shape[0]
    rows = group // 8
    z_rows = jnp.dot(features, weight, preferred_element_type=F32)
    u_rows, inv_u = unit_rows(z_rows)
    image_unit = u_rows.astype(BF)
    v_rows, _ = unit_rows(texts.astype(F32))
    text_unit = v_rows.astype(BF)
    scores = 100.0 * right_product(image_unit, text_unit)
    row_peak = jnp.max(scores, axis=1)
    col_peak = jnp.max(scores, axis=0)
    lse_row = row_peak + jnp.log(jnp.sum(jnp.exp(scores - row_peak[:, None]), axis=1))
    lse_col = col_peak + jnp.log(jnp.sum(jnp.exp(scores - col_peak[None, :]), axis=0))
    eye = (
        lax.broadcasted_iota(jnp.int32, (group, group), 0)
        == lax.broadcasted_iota(jnp.int32, (group, group), 1)
    ).astype(F32)
    diagonal = jnp.sum(scores * eye, axis=1)
    loss = jnp.sum(lse_row - diagonal) + jnp.sum(lse_col - diagonal)
    coupling = (
        jnp.exp(scores - lse_row[:, None])
        + jnp.exp(scores - lse_col[None, :])
        - 2.0 * eye
    ).astype(BF)
    du = 100.0 * jnp.dot(coupling, text_unit, preferred_element_type=F32)
    dz = ((du - u_rows * jnp.sum(u_rows * du, axis=-1, keepdims=True)) * inv_u).astype(BF)
    first = own * rows
    own_coupling = lax.dynamic_slice(coupling, (0, first), (group, rows))
    dv = 100.0 * left_product(own_coupling, image_unit)
    own_text = lax.dynamic_slice(texts, (first, 0), (rows, texts.shape[1]))
    v_own, inv_v = unit_rows(own_text.astype(F32))
    text_grad = ((dv - v_own * jnp.sum(v_own * dv, axis=-1, keepdims=True)) * inv_v).astype(BF)
    dz_own = lax.dynamic_slice(dz, (first, 0), (rows, dz.shape[1]))
    feat_grad = right_product(dz_own, weight).astype(BF)
    own_features = lax.dynamic_slice(features, (0, own * columns), (group, columns))
    head = left_product(own_features, dz)
    return loss, feat_grad, text_grad, head


def pieces(value):
    one = value.astype(BF)
    two = (value - one.astype(F32)).astype(BF)
    three = (value - one.astype(F32) - two.astype(F32)).astype(BF)
    return one, two, three


def loss_rows(loss, width):
    lane = lax.broadcasted_iota(jnp.int32, (16, width), 1)
    row = lax.broadcasted_iota(jnp.int32, (16, width), 0)
    out = jnp.zeros((16, width), BF)
    for k, piece in enumerate(pieces(loss)):
        out = jnp.where((lane == k) & (row == 0), piece, out)
    return out


def sum_over_groups(head, loss, n_h, n_z):
    rows, width = head.shape
    core = lax.axis_index("core")
    padded = -(-rows // 16) * 16
    half = width // 2
    top = jnp.pad(head, ((0, padded - rows), (0, 0))).astype(BF)
    first, second = top[:, :half], top[:, half:]
    tail = loss_rows(loss, half)
    mine = jnp.where(core == 0, first, second)
    other = jnp.where(core == 0, second, first)
    other = jnp.concatenate([other, tail], axis=0)
    came = lax.ppermute(other, "core", [(0, 1), (1, 0)])
    both = (mine.astype(F32) + came[:padded].astype(F32)).astype(BF)
    chip_loss = loss + jnp.sum(came[padded].astype(F32)[:3])
    both = jnp.concatenate([both, loss_rows(chip_loss, half)], axis=0)
    lanes = half // 128
    groups = both.shape[0] // 16
    tiles = both.reshape(groups, 16, lanes, 128).transpose(0, 2, 1, 3).reshape(-1, 16, 128)
    peers = n_h * n_z
    count = tiles.shape[0]
    each = -(-count // peers)
    tiles = jnp.pad(tiles, ((0, each * peers - count), (0, 0), (0, 0)))
    tiles = lax.all_to_all(tiles, ("yh", "z"), 0, 0, tiled=True)
    total = jnp.sum(tiles.reshape(peers, each, 16, 128).astype(F32), axis=0)
    loss_tile = count - lanes
    place = (lax.axis_index("yh") * n_z + lax.axis_index("z")) * each
    here = (place + lax.broadcasted_iota(jnp.int32, (each, 16, 128), 0)) == loss_tile
    row = lax.broadcasted_iota(jnp.int32, (each, 16, 128), 1)
    one, two, three = pieces(total[:, :1])
    send = total.astype(BF)
    send = jnp.where(here & (row == 1), two, send)
    send = jnp.where(here & (row == 2), three, send)
    send = jnp.broadcast_to(send[None], (peers, each, 16, 128)).reshape(-1, 16, 128)
    tiles = lax.all_to_all(send, ("yh", "z"), 0, 0, tiled=True)
    loss = jnp.sum(tiles[loss_tile][:3, :3].astype(F32))
    tiles = tiles[: (padded // 16) * lanes].reshape(padded // 16, lanes, 16, 128)
    part = tiles.transpose(0, 2, 1, 3).reshape(padded, half)
    whole = lax.all_gather(part, "core", axis=1, tiled=True)
    return whole[:rows].astype(F32), loss


def solution(mesh):
    n_dp, n_fs = mesh.devices.shape
    n_x, n_y = 4, 2
    n_h = 4 if n_dp % 8 == 0 else 1
    n_z = n_dp // (2 * n_h)
    fine = Mesh(
        mesh.devices.reshape(n_h, n_z, 2, n_y, n_x), ("yh", "z", "core", "yl", "x")
    )
    every = ("yh", "z", "core", "yl", "x")
    part = ("yl", "x")

    def body(features, head_weight, text_embed):
        rows, depth = features.shape
        width = text_embed.shape[1]
        weight = lax.all_gather(head_weight, part, axis=0, tiled=True)
        packed = jnp.concatenate([text_embed, features], axis=1)
        packed = jnp.pad(packed, ((0, 0), (0, -packed.shape[1] % 128)))
        got = gather_group(packed, n_y, n_x)
        y, x = lax.axis_index("yl"), lax.axis_index("x")
        texts = jnp.zeros((n_fs * rows, width), BF)
        all_features = jnp.zeros((n_fs * rows, depth), BF)
        for (dy, dx), block in got.items():
            place = (((y + dy) % n_y) * n_x + (x + dx) % n_x) * rows
            texts = lax.dynamic_update_slice(texts, block[:, :width], (place, 0))
            all_features = lax.dynamic_update_slice(
                all_features, block[:, width : width + depth], (place, 0)
            )
        own = y * n_x + x
        loss, feat_grad, text_grad, head = compute(
            weight, all_features, texts, own, head_weight.shape[0]
        )
        head_grad, loss = sum_over_groups(head, loss, n_h, n_z)
        loss = loss / (2.0 * n_fs * rows * n_dp)
        return (loss, feat_grad, text_grad, head_grad)

    in_specs = (P(every, None), P(part, None), P(every, None))
    out_specs = (P(), P(every, None), P(every, None), P(part, None))
    return jax.shard_map(
        body, mesh=fine, in_specs=in_specs, out_specs=out_specs, check_vma=False
    )
```

```python
import functools

import jax
import jax.numpy as jnp
from jax import lax
from jax.experimental import pallas as pl
from jax.experimental.pallas import tpu as pltpu
from jax.sharding import Mesh, PartitionSpec as P

BF = jnp.bfloat16
F32 = jnp.float32
LOG2E = 1.4426950408889634
LN2 = 0.6931471805599453
CHUNK = 128
NT = (((1,), (1,)), ((), ()))
TN = (((0,), (0,)), ((), ()))


def spans(size, step):
    return [(at, min(step, size - at)) for at in range(0, size, step)]


def group_kernel(n_fs, depth, place_ref, weight_ref, *refs):
    blocks = refs[: n_fs + 1]
    head_ref, loss_ref, unit_out, coupling_out, dz_out = refs[n_fs + 1 : n_fs + 6]
    packed, weight, u_full, inv_u, unit, text, score, prob, coupling, dz, dg, sems, wsem, osem = refs[n_fs + 6 :]
    group, width = unit.shape
    rows = group // n_fs
    padded = weight.shape[0]
    own = place_ref[0]
    copies = []
    for k in range(n_fs - 1):
        at = pl.multiple_of(place_ref[k] * rows, 16)
        copies.append(pltpu.make_async_copy(blocks[k], packed.at[pl.ds(at, rows)], sems.at[k]))
    cut = blocks[n_fs - 1].shape[0]
    at = pl.multiple_of(place_ref[n_fs - 1] * rows, 16)
    copies.append(pltpu.make_async_copy(blocks[n_fs - 1], packed.at[pl.ds(at, cut)], sems.at[n_fs - 1]))
    copies.append(pltpu.make_async_copy(blocks[n_fs], packed.at[pl.ds(at + cut, rows - cut)], sems.at[n_fs]))
    copies.append(pltpu.make_async_copy(weight_ref, weight.at[pl.ds(0, depth)], wsem))
    for copy in copies:
        copy.start()
    weight[depth:, :] = jnp.zeros((padded - depth, width), BF)
    dg[...] = jnp.zeros_like(dg)
    for copy in copies:
        copy.wait()

    for at, size in spans(width, 256):
        u_full[:, at : at + size] = jnp.dot(
            packed[:, width:], weight[:, at : at + size], preferred_element_type=F32
        )

    def normalise(k, carry):
        r = pl.ds(pl.multiple_of(k * CHUNK, CHUNK), CHUNK)
        z = u_full[r, :]
        inverse = lax.rsqrt(jnp.sum(z * z, axis=1, keepdims=True) + 1e-06)
        u = z * inverse
        u_full[r, :] = u
        unit[r, :] = u.astype(BF)
        inv_u[r, :] = jnp.broadcast_to(inverse, (CHUNK, 128))
        t = packed[r, :width].astype(F32)
        inverse = lax.rsqrt(jnp.sum(t * t, axis=1, keepdims=True) + 1e-06)
        text[r, :] = (t * inverse).astype(BF)
        return carry

    lax.fori_loop(0, group // CHUNK, normalise, 0)
    out_unit = pltpu.make_async_copy(unit, unit_out, osem.at[0])
    out_unit.start()

    for at, size in spans(group, 256):
        score[:, at : at + size] = lax.dot_general(
            unit[...], text[at : at + size, :], NT, preferred_element_type=F32
        )

    lane = lax.broadcasted_iota(jnp.int32, (CHUNK, 128), 1)
    line = lax.broadcasted_iota(jnp.int32, (CHUNK, 128), 0)

    def window(k):
        at = k * CHUNK
        left = at // 128 * 128
        return pl.ds(pl.multiple_of(left, 128), 128), (lane - line) == (at - left)

    def tiles(values):
        return values.reshape(CHUNK // 8, 8, values.shape[1])

    def by_row(k, carry):
        peak, terms = carry
        r = pl.ds(pl.multiple_of(k * CHUNK, CHUNK), CHUNK)
        s = score[r, :] * (100.0 * LOG2E)
        score[r, :] = s
        m = jnp.max(s, axis=1, keepdims=True)
        p = jnp.exp2(s - m)
        total = jnp.sum(p, axis=1, keepdims=True)
        prob[r, :] = p * (1.0 / total)
        cols, eye = window(k)
        diagonal = jnp.where(eye, score[r, cols], 0.0)
        dg[:, cols] += jnp.sum(tiles(diagonal), axis=0)
        term = m + jnp.log2(total) - jnp.sum(diagonal, axis=1, keepdims=True)
        return jnp.maximum(peak, jnp.max(tiles(s), axis=0)), terms + term

    peak, row_terms = lax.fori_loop(
        0,
        group // CHUNK,
        by_row,
        (jnp.full((8, group), -jnp.inf, F32), jnp.zeros((CHUNK, 1), F32)),
    )
    peak = jnp.max(peak, axis=0, keepdims=True)

    def by_col(k, total):
        r = pl.ds(pl.multiple_of(k * CHUNK, CHUNK), CHUNK)
        q = jnp.exp2(score[r, :] - peak)
        score[r, :] = q
        return total + jnp.sum(tiles(q), axis=0)

    total = lax.fori_loop(0, group // CHUNK, by_col, jnp.zeros((8, group), F32))
    total = jnp.sum(total, axis=0, keepdims=True)
    col_terms = peak + jnp.log2(total) - jnp.sum(dg[...], axis=0, keepdims=True)
    loss = LN2 * (jnp.sum(row_terms) + jnp.sum(col_terms))
    loss_ref[...] = jnp.full(loss_ref.shape, loss, F32)
    dg[0:1, :] = 1.0 / total

    def couple(k, carry):
        r = pl.ds(pl.multiple_of(k * CHUNK, CHUNK), CHUNK)
        coupling[r, :] = (prob[r, :] + score[r, :] * dg[0:1, :]).astype(BF)
        cols, eye = window(k)
        c = prob[r, cols] + score[r, cols] * dg[0:1, cols]
        coupling[r, cols] = (c - jnp.where(eye, 2.0, 0.0)).astype(BF)
        return carry

    lax.fori_loop(0, group // CHUNK, couple, 0)
    out_coupling = pltpu.make_async_copy(coupling, coupling_out, osem.at[1])
    out_coupling.start()

    for at, size in spans(width, 256):
        prob[:, at : at + size] = jnp.dot(
            coupling[...], text[:, at : at + size], preferred_element_type=F32
        )

    def to_dz(k, carry):
        r = pl.ds(pl.multiple_of(k * CHUNK, CHUNK), CHUNK)
        du = 100.0 * prob[r, :width]
        u = u_full[r, :]
        along = jnp.sum(u * du, axis=1, keepdims=True)
        dz[r, :] = ((du - u * along) * inv_u[r, 0:1]).astype(BF)
        return carry

    lax.fori_loop(0, group // CHUNK, to_dz, 0)
    mine = dz.at[pl.ds(pl.multiple_of(own * rows, 16), rows)]
    out_dz = pltpu.make_async_copy(mine, dz_out, osem.at[2])
    out_dz.start()

    columns = depth // n_fs
    pick = (
        lax.broadcasted_iota(jnp.int32, (padded, 128), 0)
        == own * columns + lax.broadcasted_iota(jnp.int32, (padded, 128), 1)
    ) & (lax.broadcasted_iota(jnp.int32, (padded, 128), 1) < columns)
    features = jnp.dot(
        packed[:, width:], pick.astype(F32).astype(BF), preferred_element_type=F32
    ).astype(BF)
    head = lax.dot_general(features, dz[...], TN, preferred_element_type=F32)
    head_ref[...] = head[: head_ref.shape[0], :].astype(BF)
    out_unit.wait()
    out_coupling.wait()
    out_dz.wait()


def group_call(place, weight, blocks, depth):
    n_fs = len(blocks) - 1
    rows, lanes = blocks[0].shape
    width = weight.shape[1]
    group = n_fs * rows
    padded = lanes - width
    head_rows = -(-(depth // n_fs) // 16) * 16
    anywhere = pl.BlockSpec(memory_space=pl.ANY)
    inside = pl.BlockSpec(memory_space=pltpu.VMEM)
    return pl.pallas_call(
        functools.partial(group_kernel, n_fs, depth),
        out_shape=(
            jax.ShapeDtypeStruct((head_rows, width), BF),
            jax.ShapeDtypeStruct((8, 128), F32),
            jax.ShapeDtypeStruct((group, width), BF),
            jax.ShapeDtypeStruct((group, group), BF),
            jax.ShapeDtypeStruct((rows, width), BF),
        ),
        in_specs=[pl.BlockSpec(memory_space=pltpu.SMEM)] + [anywhere] * (len(blocks) + 1),
        out_specs=(inside, inside, anywhere, anywhere, anywhere),
        scratch_shapes=[
            pltpu.VMEM((group, lanes), BF),
            pltpu.VMEM((padded, width), BF),
            pltpu.VMEM((group, width), F32),
            pltpu.VMEM((group, 128), F32),
            pltpu.VMEM((group, width), BF),
            pltpu.VMEM((group, width), BF),
            pltpu.VMEM((group, group), F32),
            pltpu.VMEM((group, group), F32),
            pltpu.VMEM((group, group), BF),
            pltpu.VMEM((group, width), BF),
            pltpu.VMEM((8, group), F32),
            pltpu.SemaphoreType.DMA((n_fs + 1,)),
            pltpu.SemaphoreType.DMA,
            pltpu.SemaphoreType.DMA((3,)),
        ],
        compiler_params=pltpu.CompilerParams(vmem_limit_bytes=60 * 1024 * 1024),
        cost_estimate=pl.CostEstimate(
            flops=12 * 10**9, bytes_accessed=20 * 10**6, transcendentals=4 * 10**6
        ),
        name="group",
    )(place, weight, *blocks)


def left_product(left, right):
    return lax.dot_general(
        left, right, (((0,), (0,)), ((), ())), preferred_element_type=F32
    )


def right_product(left, right):
    return lax.dot_general(
        left, right, (((1,), (1,)), ((), ())), preferred_element_type=F32
    )


def unit_rows(vectors):
    inverse = lax.rsqrt(jnp.sum(vectors * vectors, axis=-1, keepdims=True) + 1e-06)
    return (vectors * inverse, inverse)


def ring(size, step):
    return [(i, (i + step) % size) for i in range(size)]


def gather_group(block, n_y, n_x):
    flip, up, down = ring(n_y, 1), ring(n_x, 1), ring(n_x, -1)
    rows = block.shape[0]
    half = rows // 2 // 16 * 16
    got = {(0, 0): block}
    got[1, 0] = lax.ppermute(block, "yl", flip)
    got[0, 3] = lax.ppermute(block, "x", up)
    got[0, 1] = lax.ppermute(block, "x", down)
    got[1, 3] = lax.ppermute(got[0, 3], "yl", flip)
    got[1, 1] = lax.ppermute(got[1, 0], "x", down)
    got[0, 2] = lax.ppermute(got[0, 3], "x", up)
    low = lax.ppermute(got[1, 3][:half], "x", up)
    high = lax.ppermute(got[1, 1][half:], "x", down)
    keys = list(got) + [(1, 2)]
    return keys, list(got.values()) + [low, high]


def gather_head(head_weight, part, n_fs):
    rows, width = head_weight.shape
    half = width // 2
    core = lax.axis_index("core")
    mine = jnp.where(core == 0, head_weight[:, :half], head_weight[:, half:])
    mine = jnp.broadcast_to(mine[None], (n_fs, rows, half))
    mine = lax.all_to_all(mine, part, 0, 0, tiled=True).reshape(n_fs * rows, half)
    other = lax.ppermute(mine, "core", [(0, 1), (1, 0)])
    left = jnp.where(core == 0, mine, other)
    right = jnp.where(core == 0, other, mine)
    return jnp.concatenate([left, right], axis=1)


def pieces(value):
    one = value.astype(BF)
    two = (value - one.astype(F32)).astype(BF)
    three = (value - one.astype(F32) - two.astype(F32)).astype(BF)
    return one, two, three


def loss_rows(loss, width):
    lane = lax.broadcasted_iota(jnp.int32, (16, width), 1)
    row = lax.broadcasted_iota(jnp.int32, (16, width), 0)
    out = jnp.zeros((16, width), BF)
    for k, piece in enumerate(pieces(loss)):
        out = jnp.where((lane == k) & (row == 0), piece, out)
    return out


def sum_over_groups(head, loss, n_h, n_z):
    padded, width = head.shape
    core = lax.axis_index("core")
    half = width // 2
    first, second = head[:, :half], head[:, half:]
    tail = loss_rows(loss, half)
    mine = jnp.where(core == 0, first, second)
    other = jnp.where(core == 0, second, first)
    other = jnp.concatenate([other, tail], axis=0)
    came = lax.ppermute(other, "core", [(0, 1), (1, 0)])
    both = (mine.astype(F32) + came[:padded].astype(F32)).astype(BF)
    chip_loss = loss + jnp.sum(came[padded].astype(F32)[:3])
    both = jnp.concatenate([both, loss_rows(chip_loss, half)], axis=0)
    lanes = half // 128
    groups = both.shape[0] // 16
    tiles = both.reshape(groups, 16, lanes, 128).transpose(0, 2, 1, 3).reshape(-1, 16, 128)
    peers = n_h * n_z
    count = tiles.shape[0]
    each = -(-count // peers)
    tiles = jnp.pad(tiles, ((0, each * peers - count), (0, 0), (0, 0)))
    tiles = lax.all_to_all(tiles, ("yh", "z"), 0, 0, tiled=True)
    total = jnp.sum(tiles.reshape(peers, each, 16, 128).astype(F32), axis=0)
    loss_tile = count - lanes
    place = (lax.axis_index("yh") * n_z + lax.axis_index("z")) * each
    here = (place + lax.broadcasted_iota(jnp.int32, (each, 16, 128), 0)) == loss_tile
    row = lax.broadcasted_iota(jnp.int32, (each, 16, 128), 1)
    one, two, three = pieces(total[:, :1])
    send = total.astype(BF)
    send = jnp.where(here & (row == 1), two, send)
    send = jnp.where(here & (row == 2), three, send)
    send = jnp.broadcast_to(send[None], (peers, each, 16, 128)).reshape(-1, 16, 128)
    tiles = lax.all_to_all(send, ("yh", "z"), 0, 0, tiled=True)
    loss = jnp.sum(tiles[loss_tile][:3, :3].astype(F32))
    tiles = tiles[: (padded // 16) * lanes].reshape(padded // 16, lanes, 16, 128)
    part = tiles.transpose(0, 2, 1, 3).reshape(padded, half)
    whole = lax.all_gather(part, "core", axis=1, tiled=True)
    return whole.astype(F32), loss


def solution(mesh):
    n_dp, n_fs = mesh.devices.shape
    n_x, n_y = 4, 2
    n_h = 4 if n_dp % 8 == 0 else 1
    n_z = n_dp // (2 * n_h)
    fine = Mesh(
        mesh.devices.reshape(n_h, n_z, 2, n_y, n_x), ("yh", "z", "core", "yl", "x")
    )
    every = ("yh", "z", "core", "yl", "x")
    part = ("yl", "x")

    def body(features, head_weight, text_embed):
        rows, depth = features.shape
        width = text_embed.shape[1]
        weight = gather_head(head_weight, part, n_fs)
        packed = jnp.concatenate([text_embed, features], axis=1)
        packed = jnp.pad(packed, ((0, 0), (0, -packed.shape[1] % 128)))
        keys, blocks = gather_group(packed, n_y, n_x)
        y, x = lax.axis_index("yl"), lax.axis_index("x")
        place = jnp.stack(
            [((y + dy) % n_y) * n_x + (x + dx) % n_x for dy, dx in keys]
        ).astype(jnp.int32)
        head, loss, image_unit, coupling, dz = group_call(place, weight, blocks, depth)
        own_coupling = lax.dynamic_slice(
            coupling, (0, place[0] * rows), (n_fs * rows, rows)
        )
        dv = 100.0 * left_product(own_coupling, image_unit)
        v_rows, inv_v = unit_rows(text_embed.astype(F32))
        text_grad = (
            (dv - v_rows * jnp.sum(v_rows * dv, axis=-1, keepdims=True)) * inv_v
        ).astype(BF)
        feat_grad = right_product(dz, weight).astype(BF)
        head_grad, loss = sum_over_groups(head, loss[0, 0], n_h, n_z)
        head_grad = head_grad[: head_weight.shape[0]]
        loss = loss / (2.0 * n_fs * rows * n_dp)
        return (loss, feat_grad, text_grad, head_grad)

    in_specs = (P(every, None), P(part, None), P(every, None))
    out_specs = (P(), P(every, None), P(every, None), P(part, None))
    return jax.shard_map(
        body, mesh=fine, in_specs=in_specs, out_specs=out_specs, check_vma=False
    )
```

```python
import functools

import jax
import jax.numpy as jnp
from jax import lax
from jax.experimental import pallas as pl
from jax.experimental.pallas import tpu as pltpu
from jax.sharding import Mesh, PartitionSpec as P

BF = jnp.bfloat16
F32 = jnp.float32
LOG2E = 1.4426950408889634
LN2 = 0.6931471805599453
CHUNK = 128
NT = (((1,), (1,)), ((), ()))
TN = (((0,), (0,)), ((), ()))


def spans(size, step):
    return [(at, min(step, size - at)) for at in range(0, size, step)]


def put_pieces(out_ref, at, value):
    lane = lax.broadcasted_iota(jnp.int32, (16, 128), 1)
    line = lax.broadcasted_iota(jnp.int32, (16, 128), 0)
    value = jnp.broadcast_to(value[0:1, :], (16, 128))
    one = value.astype(BF).astype(F32)
    two = (value - one).astype(BF).astype(F32)
    three = value - one - two
    row = jnp.where(lane == 0, one, jnp.where(lane == 1, two, three))
    row = jnp.where((line == 0) & (lane < 3), row, 0.0)
    out_ref[at : at + 16, 0:128] = row.astype(BF)
    if out_ref.shape[1] > 128:
        out_ref[at : at + 16, 128:] = jnp.zeros((16, out_ref.shape[1] - 128), BF)


def group_kernel(n_fs, depth, layout, place_ref, weight_ref, *refs):
    blocks, refs = refs[: len(layout)], refs[len(layout) :]
    mine_ref, other_ref, loss_ref, unit_out, coupling_out, dz_out = refs[:6]
    feats, words, weight, u_full, inv_u, unit, text, score, prob, coupling, dz, dg, fsem, tsem, wsem, osem = refs[6:]
    group, width = unit.shape
    rows = group // n_fs
    padded = weight.shape[0]
    own = place_ref[0]
    copies = []
    for k, (slot, down) in enumerate(layout):
        first = pl.multiple_of(place_ref[slot] * rows + down, 16)
        at = pl.ds(first, blocks[k].shape[0])
        source = blocks[k].at[:, pl.ds(width, padded)]
        copies.append(pltpu.make_async_copy(source, feats.at[at], fsem.at[k]))
        source = blocks[k].at[:, pl.ds(0, width)]
        copies.append(pltpu.make_async_copy(source, words.at[at], tsem.at[k]))
    copies.append(pltpu.make_async_copy(weight_ref, weight.at[pl.ds(0, depth)], wsem))
    for copy in copies:
        copy.start()
    weight[depth:, :] = jnp.zeros((padded - depth, width), BF)
    dg[...] = jnp.zeros_like(dg)
    for copy in copies:
        copy.wait()

    for at, size in spans(width, 256):
        u_full[:, at : at + size] = jnp.dot(
            feats[...], weight[:, at : at + size], preferred_element_type=F32
        )

    def normalise(k, carry):
        r = pl.ds(pl.multiple_of(k * CHUNK, CHUNK), CHUNK)
        z = u_full[r, :]
        inverse = lax.rsqrt(jnp.sum(z * z, axis=1, keepdims=True) + 1e-06)
        u = z * inverse
        u_full[r, :] = u
        unit[r, :] = u.astype(BF)
        inv_u[r, :] = jnp.broadcast_to(inverse, (CHUNK, 128))
        t = words[r, :].astype(F32)
        inverse = lax.rsqrt(jnp.sum(t * t, axis=1, keepdims=True) + 1e-06)
        text[r, :] = (t * inverse).astype(BF)
        return carry

    lax.fori_loop(0, group // CHUNK, normalise, 0)
    out_unit = pltpu.make_async_copy(unit, unit_out, osem.at[0])
    out_unit.start()

    for at, size in spans(group, 256):
        score[:, at : at + size] = lax.dot_general(
            unit[...], text[at : at + size, :], NT, preferred_element_type=F32
        )

    lane = lax.broadcasted_iota(jnp.int32, (CHUNK, 128), 1)
    line = lax.broadcasted_iota(jnp.int32, (CHUNK, 128), 0)

    def window(k):
        at = k * CHUNK
        left = at // 128 * 128
        return pl.ds(pl.multiple_of(left, 128), 128), (lane - line) == (at - left)

    def tiles(values):
        return values.reshape(CHUNK // 8, 8, values.shape[1])

    def by_row(k, carry):
        peak, terms = carry
        r = pl.ds(pl.multiple_of(k * CHUNK, CHUNK), CHUNK)
        s = score[r, :] * (100.0 * LOG2E)
        score[r, :] = s
        m = jnp.max(s, axis=1, keepdims=True)
        p = jnp.exp2(s - m)
        total = jnp.sum(p, axis=1, keepdims=True)
        prob[r, :] = p * (1.0 / total)
        cols, eye = window(k)
        diagonal = jnp.where(eye, score[r, cols], 0.0)
        dg[:, cols] += jnp.sum(tiles(diagonal), axis=0)
        term = m + jnp.log2(total) - jnp.sum(diagonal, axis=1, keepdims=True)
        return jnp.maximum(peak, jnp.max(tiles(s), axis=0)), terms + term

    peak, row_terms = lax.fori_loop(
        0,
        group // CHUNK,
        by_row,
        (jnp.full((8, group), -jnp.inf, F32), jnp.zeros((CHUNK, 1), F32)),
    )
    peak = jnp.max(peak, axis=0, keepdims=True)

    def by_col(k, total):
        r = pl.ds(pl.multiple_of(k * CHUNK, CHUNK), CHUNK)
        q = jnp.exp2(score[r, :] - peak)
        score[r, :] = q
        return total + jnp.sum(tiles(q), axis=0)

    total = lax.fori_loop(0, group // CHUNK, by_col, jnp.zeros((8, group), F32))
    total = jnp.sum(total, axis=0, keepdims=True)
    col_terms = peak + jnp.log2(total) - jnp.sum(dg[...], axis=0, keepdims=True)
    loss = LN2 * (jnp.sum(row_terms) + jnp.sum(col_terms))
    loss_ref[...] = jnp.full(loss_ref.shape, loss, F32)
    dg[0:1, :] = 1.0 / total

    def couple(k, carry):
        r = pl.ds(pl.multiple_of(k * CHUNK, CHUNK), CHUNK)
        coupling[r, :] = (prob[r, :] + score[r, :] * dg[0:1, :]).astype(BF)
        cols, eye = window(k)
        c = prob[r, cols] + score[r, cols] * dg[0:1, cols]
        coupling[r, cols] = (c - jnp.where(eye, 2.0, 0.0)).astype(BF)
        return carry

    lax.fori_loop(0, group // CHUNK, couple, 0)
    out_coupling = pltpu.make_async_copy(coupling, coupling_out, osem.at[1])
    out_coupling.start()

    for at, size in spans(width, 256):
        prob[:, at : at + size] = jnp.dot(
            coupling[...], text[:, at : at + size], preferred_element_type=F32
        )

    def to_dz(k, carry):
        r = pl.ds(pl.multiple_of(k * CHUNK, CHUNK), CHUNK)
        du = 100.0 * prob[r, :width]
        u = u_full[r, :]
        along = jnp.sum(u * du, axis=1, keepdims=True)
        dz[r, :] = ((du - u * along) * inv_u[r, 0:1]).astype(BF)
        return carry

    lax.fori_loop(0, group // CHUNK, to_dz, 0)
    mine = dz.at[pl.ds(pl.multiple_of(own * rows, 16), rows)]
    out_dz = pltpu.make_async_copy(mine, dz_out, osem.at[2])
    out_dz.start()

    columns = depth // n_fs
    pick = (
        lax.broadcasted_iota(jnp.int32, (padded, 128), 0)
        == own * columns + lax.broadcasted_iota(jnp.int32, (padded, 128), 1)
    ) & (lax.broadcasted_iota(jnp.int32, (padded, 128), 1) < columns)
    features = jnp.dot(
        feats[...], pick.astype(F32).astype(BF), preferred_element_type=F32
    ).astype(BF)
    head = lax.dot_general(features, dz[...], TN, preferred_element_type=F32)
    u_full[0:128, :] = head
    core = place_ref[n_fs]
    half = width // 2
    head_rows = mine_ref.shape[0]
    mine = pl.ds(pl.multiple_of(core * half, 128), half)
    other = pl.ds(pl.multiple_of((1 - core) * half, 128), half)
    mine_ref[...] = u_full[0:head_rows, mine]
    other_ref[0:head_rows, :] = u_full[0:head_rows, other].astype(BF)
    put_pieces(other_ref, head_rows, loss_ref[...])
    out_unit.wait()
    out_coupling.wait()
    out_dz.wait()


def group_call(place, weight, blocks, layout):
    n_fs = place.shape[0] - 1
    rows, width = blocks[0].shape[0], weight.shape[1]
    depth = weight.shape[0]
    group = n_fs * rows
    padded = -(-depth // 128) * 128
    half = width // 2
    head_rows = -(-(depth // n_fs) // 16) * 16
    anywhere = pl.BlockSpec(memory_space=pl.ANY)
    inside = pl.BlockSpec(memory_space=pltpu.VMEM)
    return pl.pallas_call(
        functools.partial(group_kernel, n_fs, depth, layout),
        out_shape=(
            jax.ShapeDtypeStruct((head_rows, half), F32),
            jax.ShapeDtypeStruct((head_rows + 16, half), BF),
            jax.ShapeDtypeStruct((8, 128), F32),
            jax.ShapeDtypeStruct((group, width), BF),
            jax.ShapeDtypeStruct((group, group), BF),
            jax.ShapeDtypeStruct((rows, width), BF),
        ),
        in_specs=[pl.BlockSpec(memory_space=pltpu.SMEM)] + [anywhere] * (len(blocks) + 1),
        out_specs=(inside, inside, inside, anywhere, anywhere, anywhere),
        scratch_shapes=[
            pltpu.VMEM((group, padded), BF),
            pltpu.VMEM((group, width), BF),
            pltpu.VMEM((padded, width), BF),
            pltpu.VMEM((group, width), F32),
            pltpu.VMEM((group, 128), F32),
            pltpu.VMEM((group, width), BF),
            pltpu.VMEM((group, width), BF),
            pltpu.VMEM((group, group), F32),
            pltpu.VMEM((group, group), F32),
            pltpu.VMEM((group, group), BF),
            pltpu.VMEM((group, width), BF),
            pltpu.VMEM((8, group), F32),
            pltpu.SemaphoreType.DMA((len(blocks),)),
            pltpu.SemaphoreType.DMA((len(blocks),)),
            pltpu.SemaphoreType.DMA,
            pltpu.SemaphoreType.DMA((3,)),
        ],
        compiler_params=pltpu.CompilerParams(vmem_limit_bytes=60 * 1024 * 1024),
        cost_estimate=pl.CostEstimate(
            flops=12 * 10**9, bytes_accessed=20 * 10**6, transcendentals=4 * 10**6
        ),
        name="group",
    )(place, weight, *blocks)


def tile_kernel(mine_ref, came_ref, loss_ref, tiles_ref, pair):
    head_rows, half = mine_ref.shape
    lanes = half // 128
    pair[...] = mine_ref[...] + came_ref[0:head_rows, :].astype(F32)
    for group in range(head_rows // 16):
        for lane in range(lanes):
            tiles_ref[lanes * group + lane] = pair[
                16 * group : 16 * group + 16, 128 * lane : 128 * lane + 128
            ].astype(BF)
    count = head_rows // 16 * lanes
    tiles_ref[count + 1 :] = jnp.zeros((tiles_ref.shape[0] - count - 1, 16, 128), BF)
    theirs = came_ref[head_rows : head_rows + 16, 0:128].astype(F32)
    theirs = jnp.sum(theirs, axis=1, keepdims=True)[0:1]
    put_pieces(tiles_ref.at[count], 0, loss_ref[...] + theirs)


def tile_call(mine, came, loss, count):
    inside = pl.BlockSpec(memory_space=pltpu.VMEM)
    return pl.pallas_call(
        tile_kernel,
        out_shape=jax.ShapeDtypeStruct((count, 16, 128), BF),
        in_specs=[inside] * 3,
        out_specs=inside,
        scratch_shapes=[pltpu.VMEM(mine.shape, F32)],
        name="tiles",
    )(mine, came, loss)


def left_product(left, right):
    return lax.dot_general(
        left, right, (((0,), (0,)), ((), ())), preferred_element_type=F32
    )


def right_product(left, right):
    return lax.dot_general(
        left, right, (((1,), (1,)), ((), ())), preferred_element_type=F32
    )


def unit_rows(vectors):
    inverse = lax.rsqrt(jnp.sum(vectors * vectors, axis=-1, keepdims=True) + 1e-06)
    return (vectors * inverse, inverse)


def ring(size, step):
    return [(i, (i + step) % size) for i in range(size)]


def gather_group(block, n_y, n_x):
    flip, up, down = ring(n_y, 1), ring(n_x, 1), ring(n_x, -1)
    rows = block.shape[0]
    half = rows // 2 // 16 * 16
    got = {(0, 0): block}
    got[1, 0] = lax.ppermute(block, "yl", flip)
    got[0, 3] = lax.ppermute(block, "x", up)
    got[0, 1] = lax.ppermute(block, "x", down)
    got[1, 0], got[0, 3], got[0, 1] = lax.optimization_barrier(
        (got[1, 0], got[0, 3], got[0, 1])
    )
    got[1, 3] = lax.ppermute(got[0, 3], "yl", flip)
    got[1, 1] = lax.ppermute(got[1, 0], "x", down)
    got[0, 2] = lax.ppermute(got[0, 3], "x", up)
    low = lax.ppermute(got[1, 3][:half], "x", up)
    high = lax.ppermute(got[1, 1][half:], "x", down)
    keys = list(got) + [(1, 2)]
    layout = [(k, 0) for k in range(len(keys))] + [(len(keys) - 1, half)]
    return keys, list(got.values()) + [low, high], layout, got


def whole_head(head_weight, part, n_fs, first, later):
    rows, width = head_weight.shape
    half = width // 2
    core = lax.axis_index("core")
    mine = jnp.where(core == 0, head_weight[:, :half], head_weight[:, half:])
    mine = lax.optimization_barrier((mine, *first))[0]
    mine = jnp.broadcast_to(mine[None], (n_fs, rows, half))
    mine = lax.all_to_all(mine, part, 0, 0, tiled=True).reshape(n_fs * rows, half)
    mine = lax.optimization_barrier((mine, *later))[0]
    other = lax.ppermute(mine, "core", [(0, 1), (1, 0)])
    left = jnp.where(core == 0, mine, other)
    right = jnp.where(core == 0, other, mine)
    return jnp.concatenate([left, right], axis=1)


def pieces(value):
    one = value.astype(BF)
    two = (value - one.astype(F32)).astype(BF)
    three = (value - one.astype(F32) - two.astype(F32)).astype(BF)
    return one, two, three


def sum_over_groups(mine, other, loss, n_h, n_z):
    padded, half = mine.shape
    came = lax.ppermute(other, "core", [(0, 1), (1, 0)])
    lanes = half // 128
    peers = n_h * n_z
    loss_tile = padded // 16 * lanes
    each = -(-(loss_tile + 1) // peers)
    tiles = tile_call(mine, came, loss, each * peers)
    tiles = lax.all_to_all(tiles, ("yh", "z"), 0, 0, tiled=True)
    total = jnp.sum(tiles.reshape(peers, each, 16, 128).astype(F32), axis=0)
    place = (lax.axis_index("yh") * n_z + lax.axis_index("z")) * each
    here = (place + lax.broadcasted_iota(jnp.int32, (each, 16, 128), 0)) == loss_tile
    row = lax.broadcasted_iota(jnp.int32, (each, 16, 128), 1)
    one, two, three = pieces(total[:, :1])
    send = total.astype(BF)
    send = jnp.where(here & (row == 1), two, send)
    send = jnp.where(here & (row == 2), three, send)
    send = jnp.broadcast_to(send[None], (peers, each, 16, 128)).reshape(-1, 16, 128)
    tiles = lax.all_to_all(send, ("yh", "z"), 0, 0, tiled=True)
    loss = jnp.sum(tiles[loss_tile][:3, :3].astype(F32))
    tiles = tiles[: (padded // 16) * lanes].reshape(padded // 16, lanes, 16, 128)
    part = tiles.transpose(0, 2, 1, 3).reshape(padded, half)
    whole = lax.all_gather(part, "core", axis=1, tiled=True)
    return whole.astype(F32), loss


def solution(mesh):
    n_dp, n_fs = mesh.devices.shape
    n_x, n_y = 4, 2
    n_h = 4 if n_dp % 8 == 0 else 1
    n_z = n_dp // (2 * n_h)
    fine = Mesh(
        mesh.devices.reshape(n_h, n_z, 2, n_y, n_x), ("yh", "z", "core", "yl", "x")
    )
    every = ("yh", "z", "core", "yl", "x")
    part = ("yl", "x")

    def body(features, head_weight, text_embed):
        rows, depth = features.shape
        y, x = lax.axis_index("yl"), lax.axis_index("x")
        gap = jnp.zeros((rows, -depth % 128), BF)
        packed = jnp.concatenate([text_embed, features, gap], axis=1)
        keys, blocks, layout, got = gather_group(packed, n_y, n_x)
        place = [((y + dy) % n_y) * n_x + (x + dx) % n_x for dy, dx in keys]
        place = jnp.stack(place + [lax.axis_index("core")]).astype(jnp.int32)
        weight = whole_head(head_weight, part, n_fs, [], [])
        mine, other, loss, image_unit, coupling, dz = group_call(
            place, weight, blocks, tuple(layout)
        )
        own_coupling = lax.dynamic_slice(
            coupling, (0, place[0] * rows), (n_fs * rows, rows)
        )
        dv = 100.0 * left_product(own_coupling, image_unit)
        v_rows, inv_v = unit_rows(text_embed.astype(F32))
        text_grad = (
            (dv - v_rows * jnp.sum(v_rows * dv, axis=-1, keepdims=True)) * inv_v
        ).astype(BF)
        feat_grad = right_product(dz, weight).astype(BF)
        head_grad, loss = sum_over_groups(mine, other, loss, n_h, n_z)
        head_grad = head_grad[: head_weight.shape[0]]
        loss = loss / (2.0 * n_fs * rows * n_dp)
        return (loss, feat_grad, text_grad, head_grad)

    in_specs = (P(every, None), P(part, None), P(every, None))
    out_specs = (P(), P(every, None), P(every, None), P(part, None))
    return jax.shard_map(
        body, mesh=fine, in_specs=in_specs, out_specs=out_specs, check_vma=False
    )
```

```python
import functools

import jax
import jax.numpy as jnp
from jax import lax
from jax.experimental import pallas as pl
from jax.experimental.pallas import tpu as pltpu
from jax.sharding import Mesh, PartitionSpec as P

BF = jnp.bfloat16
F32 = jnp.float32
LOG2E = 1.4426950408889634
LN2 = 0.6931471805599453
CHUNK = 128
TALL = 352
NT = (((1,), (1,)), ((), ()))
TN = (((0,), (0,)), ((), ()))


def spans(size, step):
    return [(at, min(step, size - at)) for at in range(0, size, step)]


def put_pieces(out_ref, at, value):
    lane = lax.broadcasted_iota(jnp.int32, (16, 128), 1)
    line = lax.broadcasted_iota(jnp.int32, (16, 128), 0)
    value = jnp.broadcast_to(value[0:1, :], (16, 128))
    one = value.astype(BF).astype(F32)
    two = (value - one).astype(BF).astype(F32)
    three = value - one - two
    row = jnp.where(lane == 0, one, jnp.where(lane == 1, two, three))
    row = jnp.where((line == 0) & (lane < 3), row, 0.0)
    out_ref[at : at + 16, 0:128] = row.astype(BF)
    if out_ref.shape[1] > 128:
        out_ref[at : at + 16, 128:] = jnp.zeros((16, out_ref.shape[1] - 128), BF)


def group_kernel(n_fs, depth, layout, place_ref, weight_ref, *refs):
    blocks, refs = refs[: len(layout)], refs[len(layout) :]
    mine_ref, other_ref, loss_ref, unit_out, coupling_out, dz_out = refs[:6]
    feats, words, weight, u_full, inv_u, unit, text, score, prob, coupling, dz, dg, fsem, tsem, wsem, osem = refs[6:]
    group, width = unit.shape
    rows = group // n_fs
    padded = weight.shape[0]
    own = place_ref[0]
    copies, later = [pltpu.make_async_copy(weight_ref, weight.at[pl.ds(0, depth)], wsem)], []
    for k, (slot, down) in enumerate(layout):
        first = pl.multiple_of(place_ref[slot] * rows + down, 16)
        at = pl.ds(first, blocks[k].shape[0])
        source = blocks[k].at[:, pl.ds(width, padded)]
        copies.append(pltpu.make_async_copy(source, feats.at[at], fsem.at[k]))
        source = blocks[k].at[:, pl.ds(0, width)]
        later.append(pltpu.make_async_copy(source, words.at[at], tsem.at[k]))
    for copy in copies + later:
        copy.start()
    weight[depth:, :] = jnp.zeros((padded - depth, width), BF)
    dg[...] = jnp.zeros_like(dg)
    for copy in copies:
        copy.wait()

    for at, size in spans(width, 256):
        u_full[:, at : at + size] = jnp.dot(
            feats[...], weight[:, at : at + size], preferred_element_type=F32
        )

    for copy in later:
        copy.wait()

    def normalise(k, carry):
        r = pl.ds(pl.multiple_of(k * TALL, TALL), TALL)
        z = u_full[r, :]
        inverse = lax.rsqrt(jnp.sum(z * z, axis=1, keepdims=True) + 1e-06)
        u = z * inverse
        u_full[r, :] = u
        unit[r, :] = u.astype(BF)
        inv_u[r, :] = jnp.broadcast_to(inverse, (TALL, 128))
        t = words[r, :].astype(F32)
        inverse = lax.rsqrt(jnp.sum(t * t, axis=1, keepdims=True) + 1e-06)
        text[r, :] = (t * inverse).astype(BF)
        return carry

    lax.fori_loop(0, group // TALL, normalise, 0, unroll=True)
    out_unit = pltpu.make_async_copy(unit, unit_out, osem.at[0])
    out_unit.start()

    for at, size in spans(group, 256):
        score[:, at : at + size] = lax.dot_general(
            unit[...], text[at : at + size, :], NT, preferred_element_type=F32
        )

    lane = lax.broadcasted_iota(jnp.int32, (CHUNK, 128), 1)
    line = lax.broadcasted_iota(jnp.int32, (CHUNK, 128), 0)

    def window(k):
        at = k * CHUNK
        left = at // 128 * 128
        return pl.ds(pl.multiple_of(left, 128), 128), (lane - line) == (at - left)

    def tiles(values):
        return values.reshape(CHUNK // 8, 8, values.shape[1])

    def by_row(k, carry):
        peak, terms = carry
        r = pl.ds(pl.multiple_of(k * CHUNK, CHUNK), CHUNK)
        s = score[r, :] * (100.0 * LOG2E)
        score[r, :] = s
        m = jnp.max(s, axis=1, keepdims=True)
        p = jnp.exp2(s - m)
        total = jnp.sum(p, axis=1, keepdims=True)
        prob[r, :] = p * (1.0 / total)
        cols, eye = window(k)
        diagonal = jnp.where(eye, score[r, cols], 0.0)
        dg[:, cols] += jnp.sum(tiles(diagonal), axis=0)
        term = m + jnp.log2(total) - jnp.sum(diagonal, axis=1, keepdims=True)
        return jnp.maximum(peak, jnp.max(tiles(s), axis=0)), terms + term

    peak, row_terms = lax.fori_loop(
        0,
        group // CHUNK,
        by_row,
        (jnp.full((8, group), -jnp.inf, F32), jnp.zeros((CHUNK, 1), F32)),
        unroll=True,
    )
    peak = jnp.max(peak, axis=0, keepdims=True)

    def by_col(k, total):
        r = pl.ds(pl.multiple_of(k * CHUNK, CHUNK), CHUNK)
        q = jnp.exp2(score[r, :] - peak)
        score[r, :] = q
        return total + jnp.sum(tiles(q), axis=0)

    total = lax.fori_loop(0, group // CHUNK, by_col, jnp.zeros((8, group), F32))
    total = jnp.sum(total, axis=0, keepdims=True)
    col_terms = peak + jnp.log2(total) - jnp.sum(dg[...], axis=0, keepdims=True)
    loss = LN2 * (jnp.sum(row_terms) + jnp.sum(col_terms))
    loss_ref[...] = jnp.full(loss_ref.shape, loss, F32)
    dg[0:1, :] = 1.0 / total

    def couple(k, carry):
        r = pl.ds(pl.multiple_of(k * CHUNK, CHUNK), CHUNK)
        coupling[r, :] = (prob[r, :] + score[r, :] * dg[0:1, :]).astype(BF)
        cols, eye = window(k)
        c = prob[r, cols] + score[r, cols] * dg[0:1, cols]
        coupling[r, cols] = (c - jnp.where(eye, 2.0, 0.0)).astype(BF)
        return carry

    lax.fori_loop(0, group // CHUNK, couple, 0)
    out_coupling = pltpu.make_async_copy(coupling, coupling_out, osem.at[1])
    out_coupling.start()

    for at, size in spans(width, 256):
        prob[:, at : at + size] = jnp.dot(
            coupling[...], text[:, at : at + size], preferred_element_type=F32
        )

    def to_dz(k, carry):
        r = pl.ds(pl.multiple_of(k * TALL, TALL), TALL)
        du = 100.0 * prob[r, :width]
        u = u_full[r, :]
        along = jnp.sum(u * du, axis=1, keepdims=True)
        dz[r, :] = ((du - u * along) * inv_u[r, 0:1]).astype(BF)
        return carry

    lax.fori_loop(0, group // TALL, to_dz, 0, unroll=True)
    mine = dz.at[pl.ds(pl.multiple_of(own * rows, 16), rows)]
    out_dz = pltpu.make_async_copy(mine, dz_out, osem.at[2])
    out_dz.start()

    columns = depth // n_fs
    pick = (
        lax.broadcasted_iota(jnp.int32, (padded, 128), 0)
        == own * columns + lax.broadcasted_iota(jnp.int32, (padded, 128), 1)
    ) & (lax.broadcasted_iota(jnp.int32, (padded, 128), 1) < columns)
    features = jnp.dot(
        feats[...], pick.astype(F32).astype(BF), preferred_element_type=F32
    ).astype(BF)
    head = lax.dot_general(features, dz[...], TN, preferred_element_type=F32)
    u_full[0:128, :] = head
    core = place_ref[n_fs]
    half = width // 2
    head_rows = mine_ref.shape[0]
    mine = pl.ds(pl.multiple_of(core * half, 128), half)
    other = pl.ds(pl.multiple_of((1 - core) * half, 128), half)
    mine_ref[...] = u_full[0:head_rows, mine]
    other_ref[0:head_rows, :] = u_full[0:head_rows, other].astype(BF)
    put_pieces(other_ref, head_rows, loss_ref[...])
    out_unit.wait()
    out_coupling.wait()
    out_dz.wait()


def group_call(place, weight, blocks, layout):
    n_fs = place.shape[0] - 1
    rows, width = blocks[0].shape[0], weight.shape[1]
    depth = weight.shape[0]
    group = n_fs * rows
    padded = -(-depth // 128) * 128
    half = width // 2
    head_rows = -(-(depth // n_fs) // 16) * 16
    anywhere = pl.BlockSpec(memory_space=pl.ANY)
    inside = pl.BlockSpec(memory_space=pltpu.VMEM)
    return pl.pallas_call(
        functools.partial(group_kernel, n_fs, depth, layout),
        out_shape=(
            jax.ShapeDtypeStruct((head_rows, half), F32),
            jax.ShapeDtypeStruct((head_rows + 16, half), BF),
            jax.ShapeDtypeStruct((8, 128), F32),
            jax.ShapeDtypeStruct((group, width), BF),
            jax.ShapeDtypeStruct((group, group), BF),
            jax.ShapeDtypeStruct((rows, width), BF),
        ),
        in_specs=[pl.BlockSpec(memory_space=pltpu.SMEM)] + [anywhere] * (len(blocks) + 1),
        out_specs=(inside, inside, inside, anywhere, anywhere, anywhere),
        scratch_shapes=[
            pltpu.VMEM((group, padded), BF),
            pltpu.VMEM((group, width), BF),
            pltpu.VMEM((padded, width), BF),
            pltpu.VMEM((group, width), F32),
            pltpu.VMEM((group, 128), F32),
            pltpu.VMEM((group, width), BF),
            pltpu.VMEM((group, width), BF),
            pltpu.VMEM((group, group), F32),
            pltpu.VMEM((group, group), F32),
            pltpu.VMEM((group, group), BF),
            pltpu.VMEM((group, width), BF),
            pltpu.VMEM((8, group), F32),
            pltpu.SemaphoreType.DMA((len(blocks),)),
            pltpu.SemaphoreType.DMA((len(blocks),)),
            pltpu.SemaphoreType.DMA,
            pltpu.SemaphoreType.DMA((3,)),
        ],
        compiler_params=pltpu.CompilerParams(vmem_limit_bytes=60 * 1024 * 1024),
        cost_estimate=pl.CostEstimate(
            flops=12 * 10**9, bytes_accessed=20 * 10**6, transcendentals=4 * 10**6
        ),
        name="group",
    )(place, weight, *blocks)


def tile_kernel(mine_ref, came_ref, loss_ref, tiles_ref, pair):
    head_rows, half = mine_ref.shape
    lanes = half // 128
    pair[...] = mine_ref[...] + came_ref[0:head_rows, :].astype(F32)
    for group in range(head_rows // 16):
        for lane in range(lanes):
            tiles_ref[lanes * group + lane] = pair[
                16 * group : 16 * group + 16, 128 * lane : 128 * lane + 128
            ].astype(BF)
    count = head_rows // 16 * lanes
    tiles_ref[count + 1 :] = jnp.zeros((tiles_ref.shape[0] - count - 1, 16, 128), BF)
    theirs = came_ref[head_rows : head_rows + 16, 0:128].astype(F32)
    theirs = jnp.sum(theirs, axis=1, keepdims=True)[0:1]
    put_pieces(tiles_ref.at[count], 0, loss_ref[...] + theirs)


def tile_call(mine, came, loss, count):
    inside = pl.BlockSpec(memory_space=pltpu.VMEM)
    return pl.pallas_call(
        tile_kernel,
        out_shape=jax.ShapeDtypeStruct((count, 16, 128), BF),
        in_specs=[inside] * 3,
        out_specs=inside,
        scratch_shapes=[pltpu.VMEM(mine.shape, F32)],
        name="tiles",
    )(mine, came, loss)


def left_product(left, right):
    return lax.dot_general(
        left, right, (((0,), (0,)), ((), ())), preferred_element_type=F32
    )


def right_product(left, right):
    return lax.dot_general(
        left, right, (((1,), (1,)), ((), ())), preferred_element_type=F32
    )


def unit_rows(vectors):
    inverse = lax.rsqrt(jnp.sum(vectors * vectors, axis=-1, keepdims=True) + 1e-06)
    return (vectors * inverse, inverse)


def ring(size, step):
    return [(i, (i + step) % size) for i in range(size)]


def gather_group(block, n_y, n_x):
    flip, up, down = ring(n_y, 1), ring(n_x, 1), ring(n_x, -1)
    rows = block.shape[0]
    half = rows // 2 // 16 * 16
    got = {(0, 0): block}
    got[1, 0] = lax.ppermute(block, "yl", flip)
    got[0, 3] = lax.ppermute(block, "x", up)
    got[0, 1] = lax.ppermute(block, "x", down)
    got[1, 0], got[0, 3], got[0, 1] = lax.optimization_barrier(
        (got[1, 0], got[0, 3], got[0, 1])
    )
    got[1, 3] = lax.ppermute(got[0, 3], "yl", flip)
    got[1, 1] = lax.ppermute(got[1, 0], "x", down)
    got[0, 2] = lax.ppermute(got[0, 3], "x", up)
    low = lax.ppermute(got[1, 3][:half], "x", up)
    high = lax.ppermute(got[1, 1][half:], "x", down)
    keys = list(got) + [(1, 2)]
    layout = [(k, 0) for k in range(len(keys))] + [(len(keys) - 1, half)]
    return keys, list(got.values()) + [low, high], layout, got


def whole_head(head_weight, part, n_fs):
    rows, width = head_weight.shape
    half = width // 2
    core = lax.axis_index("core")
    mine = jnp.where(core == 0, head_weight[:, :half], head_weight[:, half:])
    mine = jnp.broadcast_to(mine[None], (n_fs, rows, half))
    mine = lax.all_to_all(mine, part, 0, 0, tiled=True).reshape(n_fs * rows, half)
    other = lax.ppermute(mine, "core", [(0, 1), (1, 0)])
    left = jnp.where(core == 0, mine, other)
    right = jnp.where(core == 0, other, mine)
    return jnp.concatenate([left, right], axis=1)


def pieces(value):
    one = value.astype(BF)
    two = (value - one.astype(F32)).astype(BF)
    three = (value - one.astype(F32) - two.astype(F32)).astype(BF)
    return one, two, three


def sum_over_groups(mine, other, loss, n_h, n_z):
    padded, half = mine.shape
    came = lax.ppermute(other, "core", [(0, 1), (1, 0)])
    lanes = half // 128
    peers = n_h * n_z
    loss_tile = padded // 16 * lanes
    each = -(-(loss_tile + 1) // peers)
    tiles = tile_call(mine, came, loss, each * peers)
    tiles = lax.all_to_all(tiles, ("yh", "z"), 0, 0, tiled=True)
    total = jnp.sum(tiles.reshape(peers, each, 16, 128).astype(F32), axis=0)
    place = (lax.axis_index("yh") * n_z + lax.axis_index("z")) * each
    here = (place + lax.broadcasted_iota(jnp.int32, (each, 16, 128), 0)) == loss_tile
    row = lax.broadcasted_iota(jnp.int32, (each, 16, 128), 1)
    one, two, three = pieces(total[:, :1])
    send = total.astype(BF)
    send = jnp.where(here & (row == 1), two, send)
    send = jnp.where(here & (row == 2), three, send)
    send = jnp.broadcast_to(send[None], (peers, each, 16, 128)).reshape(-1, 16, 128)
    tiles = lax.all_to_all(send, ("yh", "z"), 0, 0, tiled=True)
    loss = jnp.sum(tiles[loss_tile][:3, :3].astype(F32))
    tiles = tiles[: (padded // 16) * lanes].reshape(padded // 16, lanes, 16, 128)
    part = tiles.transpose(0, 2, 1, 3).reshape(padded, half)
    whole = lax.all_gather(part, "core", axis=1, tiled=True)
    return whole.astype(F32), loss


def solution(mesh):
    n_dp, n_fs = mesh.devices.shape
    n_x, n_y = 4, 2
    n_h = 4 if n_dp % 8 == 0 else 1
    n_z = n_dp // (2 * n_h)
    fine = Mesh(
        mesh.devices.reshape(n_h, n_z, 2, n_y, n_x), ("yh", "z", "core", "yl", "x")
    )
    every = ("yh", "z", "core", "yl", "x")
    part = ("yl", "x")

    def body(features, head_weight, text_embed):
        rows, depth = features.shape
        y, x = lax.axis_index("yl"), lax.axis_index("x")
        gap = jnp.zeros((rows, -depth % 128), BF)
        packed = jnp.concatenate([text_embed, features, gap], axis=1)
        keys, blocks, layout, got = gather_group(packed, n_y, n_x)
        place = [((y + dy) % n_y) * n_x + (x + dx) % n_x for dy, dx in keys]
        place = jnp.stack(place + [lax.axis_index("core")]).astype(jnp.int32)
        weight = whole_head(head_weight, part, n_fs)
        mine, other, loss, image_unit, coupling, dz = group_call(
            place, weight, blocks, tuple(layout)
        )
        own_coupling = lax.dynamic_slice(
            coupling, (0, place[0] * rows), (n_fs * rows, rows)
        )
        dv = 100.0 * left_product(own_coupling, image_unit)
        v_rows, inv_v = unit_rows(text_embed.astype(F32))
        text_grad = (
            (dv - v_rows * jnp.sum(v_rows * dv, axis=-1, keepdims=True)) * inv_v
        ).astype(BF)
        feat_grad = right_product(dz, weight).astype(BF)
        head_grad, loss = sum_over_groups(mine, other, loss, n_h, n_z)
        head_grad = head_grad[: head_weight.shape[0]]
        loss = loss / (2.0 * n_fs * rows * n_dp)
        return (loss, feat_grad, text_grad, head_grad)

    in_specs = (P(every, None), P(part, None), P(every, None))
    out_specs = (P(), P(every, None), P(every, None), P(part, None))
    return jax.shard_map(
        body, mesh=fine, in_specs=in_specs, out_specs=out_specs, check_vma=False
    )
```

```python
import functools

import jax
import jax.numpy as jnp
from jax import lax
from jax.experimental import pallas as pl
from jax.experimental.pallas import tpu as pltpu
from jax.sharding import Mesh, PartitionSpec as P

BF = jnp.bfloat16
F32 = jnp.float32
LOG2E = 1.4426950408889634
LN2 = 0.6931471805599453
CHUNK = 128
TALL = 352
NT = (((1,), (1,)), ((), ()))
TN = (((0,), (0,)), ((), ()))


def spans(size, step):
    return [(at, min(step, size - at)) for at in range(0, size, step)]


def put_pieces(out_ref, at, value):
    lane = lax.broadcasted_iota(jnp.int32, (16, 128), 1)
    line = lax.broadcasted_iota(jnp.int32, (16, 128), 0)
    value = jnp.broadcast_to(value[0:1, :], (16, 128))
    one = value.astype(BF).astype(F32)
    two = (value - one).astype(BF).astype(F32)
    three = value - one - two
    row = jnp.where(lane == 0, one, jnp.where(lane == 1, two, three))
    row = jnp.where((line == 0) & (lane < 3), row, 0.0)
    out_ref[at : at + 16, 0:128] = row.astype(BF)
    if out_ref.shape[1] > 128:
        out_ref[at : at + 16, 128:] = jnp.zeros((16, out_ref.shape[1] - 128), BF)


def group_kernel(n_fs, depth, layout, place_ref, weight_ref, *refs):
    blocks, refs = refs[: len(layout)], refs[len(layout) :]
    mine_ref, other_ref, loss_ref, unit_out, coupling_out, dz_out = refs[:6]
    feats, words, weight, u_full, inv_u, unit, text, score, prob, coupling, dz, dg, fsem, tsem, wsem, osem = refs[6:]
    group, width = unit.shape
    rows = group // n_fs
    padded = weight.shape[0]
    own = place_ref[0]
    copies, later = [pltpu.make_async_copy(weight_ref, weight.at[pl.ds(0, depth)], wsem)], []
    for k, (slot, down) in enumerate(layout):
        first = pl.multiple_of(place_ref[slot] * rows + down, 16)
        at = pl.ds(first, blocks[k].shape[0])
        source = blocks[k].at[:, pl.ds(width, padded)]
        copies.append(pltpu.make_async_copy(source, feats.at[at], fsem.at[k]))
        source = blocks[k].at[:, pl.ds(0, width)]
        later.append(pltpu.make_async_copy(source, words.at[at], tsem.at[k]))
    for copy in copies + later:
        copy.start()
    weight[depth:, :] = jnp.zeros((padded - depth, width), BF)
    dg[...] = jnp.zeros_like(dg)
    for copy in copies:
        copy.wait()

    for at, size in spans(width, 256):
        u_full[:, at : at + size] = jnp.dot(
            feats[...], weight[:, at : at + size], preferred_element_type=F32
        )

    for copy in later:
        copy.wait()

    def normalise(k, carry):
        r = pl.ds(pl.multiple_of(k * TALL, TALL), TALL)
        z = u_full[r, :]
        inverse = lax.rsqrt(jnp.sum(z * z, axis=1, keepdims=True) + 1e-06)
        u = z * inverse
        u_full[r, :] = u
        unit[r, :] = u.astype(BF)
        inv_u[r, :] = jnp.broadcast_to(inverse, (TALL, 128))
        t = words[r, :].astype(F32)
        inverse = lax.rsqrt(jnp.sum(t * t, axis=1, keepdims=True) + 1e-06)
        text[r, :] = (t * inverse).astype(BF)
        return carry

    lax.fori_loop(0, group // TALL, normalise, 0, unroll=True)
    out_unit = pltpu.make_async_copy(unit, unit_out, osem.at[0])
    out_unit.start()

    for at, size in spans(group, 256):
        score[:, at : at + size] = lax.dot_general(
            unit[...], text[at : at + size, :], NT, preferred_element_type=F32
        )

    lane = lax.broadcasted_iota(jnp.int32, (CHUNK, 128), 1)
    line = lax.broadcasted_iota(jnp.int32, (CHUNK, 128), 0)

    def window(k):
        at = k * CHUNK
        left = at // 128 * 128
        return pl.ds(pl.multiple_of(left, 128), 128), (lane - line) == (at - left)

    def tiles(values):
        return values.reshape(CHUNK // 8, 8, values.shape[1])

    def by_row(k, carry):
        peak, terms = carry
        r = pl.ds(pl.multiple_of(k * CHUNK, CHUNK), CHUNK)
        s = score[r, :] * (100.0 * LOG2E)
        score[r, :] = s
        m = jnp.max(s, axis=1, keepdims=True)
        p = jnp.exp2(s - m)
        total = jnp.sum(p, axis=1, keepdims=True)
        prob[r, :] = p * (1.0 / total)
        cols, eye = window(k)
        diagonal = jnp.where(eye, score[r, cols], 0.0)
        dg[:, cols] += jnp.sum(tiles(diagonal), axis=0)
        term = m + jnp.log2(total) - jnp.sum(diagonal, axis=1, keepdims=True)
        return jnp.maximum(peak, jnp.max(tiles(s), axis=0)), terms + term

    peak, row_terms = lax.fori_loop(
        0,
        group // CHUNK,
        by_row,
        (jnp.full((8, group), -jnp.inf, F32), jnp.zeros((CHUNK, 1), F32)),
        unroll=True,
    )
    peak = jnp.max(peak, axis=0, keepdims=True)

    def by_col(k, total):
        r = pl.ds(pl.multiple_of(k * CHUNK, CHUNK), CHUNK)
        q = jnp.exp2(score[r, :] - peak)
        score[r, :] = q
        return total + jnp.sum(tiles(q), axis=0)

    total = lax.fori_loop(
        0, group // CHUNK, by_col, jnp.zeros((8, group), F32), unroll=True
    )
    total = jnp.sum(total, axis=0, keepdims=True)
    col_terms = peak + jnp.log2(total) - jnp.sum(dg[...], axis=0, keepdims=True)
    loss = LN2 * (jnp.sum(row_terms) + jnp.sum(col_terms))
    loss_ref[...] = jnp.full(loss_ref.shape, loss, F32)
    dg[0:1, :] = 1.0 / total

    def couple(k, carry):
        r = pl.ds(pl.multiple_of(k * CHUNK, CHUNK), CHUNK)
        coupling[r, :] = (prob[r, :] + score[r, :] * dg[0:1, :]).astype(BF)
        cols, eye = window(k)
        c = prob[r, cols] + score[r, cols] * dg[0:1, cols]
        coupling[r, cols] = (c - jnp.where(eye, 2.0, 0.0)).astype(BF)
        return carry

    lax.fori_loop(0, group // CHUNK, couple, 0, unroll=True)
    out_coupling = pltpu.make_async_copy(coupling, coupling_out, osem.at[1])
    out_coupling.start()

    for at, size in spans(width, 256):
        prob[:, at : at + size] = jnp.dot(
            coupling[...], text[:, at : at + size], preferred_element_type=F32
        )

    def to_dz(k, carry):
        r = pl.ds(pl.multiple_of(k * TALL, TALL), TALL)
        du = 100.0 * prob[r, :width]
        u = u_full[r, :]
        along = jnp.sum(u * du, axis=1, keepdims=True)
        dz[r, :] = ((du - u * along) * inv_u[r, 0:1]).astype(BF)
        return carry

    lax.fori_loop(0, group // TALL, to_dz, 0, unroll=True)
    mine = dz.at[pl.ds(pl.multiple_of(own * rows, 16), rows)]
    out_dz = pltpu.make_async_copy(mine, dz_out, osem.at[2])
    out_dz.start()

    columns = depth // n_fs
    pick = (
        lax.broadcasted_iota(jnp.int32, (padded, 128), 0)
        == own * columns + lax.broadcasted_iota(jnp.int32, (padded, 128), 1)
    ) & (lax.broadcasted_iota(jnp.int32, (padded, 128), 1) < columns)
    features = jnp.dot(
        feats[...], pick.astype(F32).astype(BF), preferred_element_type=F32
    ).astype(BF)
    head = lax.dot_general(features, dz[...], TN, preferred_element_type=F32)
    u_full[0:128, :] = head
    core = place_ref[n_fs]
    half = width // 2
    head_rows = mine_ref.shape[0]
    mine = pl.ds(pl.multiple_of(core * half, 128), half)
    other = pl.ds(pl.multiple_of((1 - core) * half, 128), half)
    mine_ref[...] = u_full[0:head_rows, mine]
    other_ref[0:head_rows, :] = u_full[0:head_rows, other].astype(BF)
    put_pieces(other_ref, head_rows, loss_ref[...])
    out_unit.wait()
    out_coupling.wait()
    out_dz.wait()


def group_call(place, weight, blocks, layout):
    n_fs = place.shape[0] - 1
    rows, width = blocks[0].shape[0], weight.shape[1]
    depth = weight.shape[0]
    group = n_fs * rows
    padded = -(-depth // 128) * 128
    half = width // 2
    head_rows = -(-(depth // n_fs) // 16) * 16
    anywhere = pl.BlockSpec(memory_space=pl.ANY)
    inside = pl.BlockSpec(memory_space=pltpu.VMEM)
    return pl.pallas_call(
        functools.partial(group_kernel, n_fs, depth, layout),
        out_shape=(
            jax.ShapeDtypeStruct((head_rows, half), F32),
            jax.ShapeDtypeStruct((head_rows + 16, half), BF),
            jax.ShapeDtypeStruct((8, 128), F32),
            jax.ShapeDtypeStruct((group, width), BF),
            jax.ShapeDtypeStruct((group, group), BF),
            jax.ShapeDtypeStruct((rows, width), BF),
        ),
        in_specs=[pl.BlockSpec(memory_space=pltpu.SMEM)] + [anywhere] * (len(blocks) + 1),
        out_specs=(inside, inside, inside, anywhere, anywhere, anywhere),
        scratch_shapes=[
            pltpu.VMEM((group, padded), BF),
            pltpu.VMEM((group, width), BF),
            pltpu.VMEM((padded, width), BF),
            pltpu.VMEM((group, width), F32),
            pltpu.VMEM((group, 128), F32),
            pltpu.VMEM((group, width), BF),
            pltpu.VMEM((group, width), BF),
            pltpu.VMEM((group, group), F32),
            pltpu.VMEM((group, group), F32),
            pltpu.VMEM((group, group), BF),
            pltpu.VMEM((group, width), BF),
            pltpu.VMEM((8, group), F32),
            pltpu.SemaphoreType.DMA((len(blocks),)),
            pltpu.SemaphoreType.DMA((len(blocks),)),
            pltpu.SemaphoreType.DMA,
            pltpu.SemaphoreType.DMA((3,)),
        ],
        compiler_params=pltpu.CompilerParams(vmem_limit_bytes=60 * 1024 * 1024),
        cost_estimate=pl.CostEstimate(
            flops=12 * 10**9, bytes_accessed=20 * 10**6, transcendentals=4 * 10**6
        ),
        name="group",
    )(place, weight, *blocks)


def tile_kernel(mine_ref, came_ref, loss_ref, tiles_ref, pair):
    head_rows, half = mine_ref.shape
    lanes = half // 128
    pair[...] = mine_ref[...] + came_ref[0:head_rows, :].astype(F32)
    for group in range(head_rows // 16):
        for lane in range(lanes):
            tiles_ref[lanes * group + lane] = pair[
                16 * group : 16 * group + 16, 128 * lane : 128 * lane + 128
            ].astype(BF)
    count = head_rows // 16 * lanes
    tiles_ref[count + 1 :] = jnp.zeros((tiles_ref.shape[0] - count - 1, 16, 128), BF)
    theirs = came_ref[head_rows : head_rows + 16, 0:128].astype(F32)
    theirs = jnp.sum(theirs, axis=1, keepdims=True)[0:1]
    put_pieces(tiles_ref.at[count], 0, loss_ref[...] + theirs)


def tile_call(mine, came, loss, count):
    inside = pl.BlockSpec(memory_space=pltpu.VMEM)
    return pl.pallas_call(
        tile_kernel,
        out_shape=jax.ShapeDtypeStruct((count, 16, 128), BF),
        in_specs=[inside] * 3,
        out_specs=inside,
        scratch_shapes=[pltpu.VMEM(mine.shape, F32)],
        name="tiles",
    )(mine, came, loss)


def left_product(left, right):
    return lax.dot_general(
        left, right, (((0,), (0,)), ((), ())), preferred_element_type=F32
    )


def right_product(left, right):
    return lax.dot_general(
        left, right, (((1,), (1,)), ((), ())), preferred_element_type=F32
    )


def unit_rows(vectors):
    inverse = lax.rsqrt(jnp.sum(vectors * vectors, axis=-1, keepdims=True) + 1e-06)
    return (vectors * inverse, inverse)


def ring(size, step):
    return [(i, (i + step) % size) for i in range(size)]


def gather_group(block, n_y, n_x):
    flip, up, down = ring(n_y, 1), ring(n_x, 1), ring(n_x, -1)
    rows = block.shape[0]
    half = rows // 2 // 16 * 16
    got = {(0, 0): block}
    got[1, 0] = lax.ppermute(block, "yl", flip)
    got[0, 3] = lax.ppermute(block, "x", up)
    got[0, 1] = lax.ppermute(block, "x", down)
    got[1, 0], got[0, 3], got[0, 1] = lax.optimization_barrier(
        (got[1, 0], got[0, 3], got[0, 1])
    )
    got[1, 3] = lax.ppermute(got[0, 3], "yl", flip)
    got[1, 1] = lax.ppermute(got[1, 0], "x", down)
    got[0, 2] = lax.ppermute(got[0, 3], "x", up)
    low = lax.ppermute(got[1, 3][:half], "x", up)
    high = lax.ppermute(got[1, 1][half:], "x", down)
    keys = list(got) + [(1, 2)]
    layout = [(k, 0) for k in range(len(keys))] + [(len(keys) - 1, half)]
    return keys, list(got.values()) + [low, high], layout, got


def whole_head(head_weight, part, n_fs):
    rows, width = head_weight.shape
    half = width // 2
    core = lax.axis_index("core")
    mine = jnp.where(core == 0, head_weight[:, :half], head_weight[:, half:])
    mine = jnp.broadcast_to(mine[None], (n_fs, rows, half))
    mine = lax.all_to_all(mine, part, 0, 0, tiled=True).reshape(n_fs * rows, half)
    other = lax.ppermute(mine, "core", [(0, 1), (1, 0)])
    left = jnp.where(core == 0, mine, other)
    right = jnp.where(core == 0, other, mine)
    return jnp.concatenate([left, right], axis=1)


def pieces(value):
    one = value.astype(BF)
    two = (value - one.astype(F32)).astype(BF)
    three = (value - one.astype(F32) - two.astype(F32)).astype(BF)
    return one, two, three


def sum_over_groups(mine, other, loss, n_h, n_z):
    padded, half = mine.shape
    came = lax.ppermute(other, "core", [(0, 1), (1, 0)])
    lanes = half // 128
    peers = n_h * n_z
    loss_tile = padded // 16 * lanes
    each = -(-(loss_tile + 1) // peers)
    tiles = tile_call(mine, came, loss, each * peers)
    tiles = lax.all_to_all(tiles, ("yh", "z"), 0, 0, tiled=True)
    total = jnp.sum(tiles.reshape(peers, each, 16, 128).astype(F32), axis=0)
    place = (lax.axis_index("yh") * n_z + lax.axis_index("z")) * each
    here = (place + lax.broadcasted_iota(jnp.int32, (each, 16, 128), 0)) == loss_tile
    row = lax.broadcasted_iota(jnp.int32, (each, 16, 128), 1)
    one, two, three = pieces(total[:, :1])
    send = total.astype(BF)
    send = jnp.where(here & (row == 1), two, send)
    send = jnp.where(here & (row == 2), three, send)
    send = jnp.broadcast_to(send[None], (peers, each, 16, 128)).reshape(-1, 16, 128)
    tiles = lax.all_to_all(send, ("yh", "z"), 0, 0, tiled=True)
    loss = jnp.sum(tiles[loss_tile][:3, :3].astype(F32))
    tiles = tiles[: (padded // 16) * lanes].reshape(padded // 16, lanes, 16, 128)
    part = tiles.transpose(0, 2, 1, 3).reshape(padded, half)
    whole = lax.all_gather(part, "core", axis=1, tiled=True)
    return whole.astype(F32), loss


def solution(mesh):
    n_dp, n_fs = mesh.devices.shape
    n_x, n_y = 4, 2
    n_h = 4 if n_dp % 8 == 0 else 1
    n_z = n_dp // (2 * n_h)
    fine = Mesh(
        mesh.devices.reshape(n_h, n_z, 2, n_y, n_x), ("yh", "z", "core", "yl", "x")
    )
    every = ("yh", "z", "core", "yl", "x")
    part = ("yl", "x")

    def body(features, head_weight, text_embed):
        rows, depth = features.shape
        y, x = lax.axis_index("yl"), lax.axis_index("x")
        gap = jnp.zeros((rows, -depth % 128), BF)
        packed = jnp.concatenate([text_embed, features, gap], axis=1)
        keys, blocks, layout, got = gather_group(packed, n_y, n_x)
        place = [((y + dy) % n_y) * n_x + (x + dx) % n_x for dy, dx in keys]
        place = jnp.stack(place + [lax.axis_index("core")]).astype(jnp.int32)
        weight = whole_head(head_weight, part, n_fs)
        mine, other, loss, image_unit, coupling, dz = group_call(
            place, weight, blocks, tuple(layout)
        )
        own_coupling = lax.dynamic_slice(
            coupling, (0, place[0] * rows), (n_fs * rows, rows)
        )
        dv = 100.0 * left_product(own_coupling, image_unit)
        v_rows, inv_v = unit_rows(text_embed.astype(F32))
        text_grad = (
            (dv - v_rows * jnp.sum(v_rows * dv, axis=-1, keepdims=True)) * inv_v
        ).astype(BF)
        feat_grad = right_product(dz, weight).astype(BF)
        head_grad, loss = sum_over_groups(mine, other, loss, n_h, n_z)
        head_grad = head_grad[: head_weight.shape[0]]
        loss = loss / (2.0 * n_fs * rows * n_dp)
        return (loss, feat_grad, text_grad, head_grad)

    in_specs = (P(every, None), P(part, None), P(every, None))
    out_specs = (P(), P(every, None), P(every, None), P(part, None))
    return jax.shard_map(
        body, mesh=fine, in_specs=in_specs, out_specs=out_specs, check_vma=False
    )
```
